32 devices in a mesh: band: 4 (over y, x), space: 8 (over z, core).
Axes of the slice: x: 2, y: 2, z: 4, core: 2. Of those that a mesh axis runs over, the one named last changes fastest.
Arguments:
- orbitals: float32 [4, 192, 192, 192], P('band', 'space'), may hold values from -6 to 6
- occupations: int32 [4], replicated, may hold values from 1 to 4
Outputs:
- exchange_potential: float32 [4, 192, 192, 192], P('band', 'space')
The draws below stay inside these ranges and needn't reach their ends.
All inputs are finite; a program needn't handle non-finite values.
Results may differ from the reference program's by a relative error of at most 0.0003.
Values sent between devices are 32-bit elements; how exact they have to be, the bound alone decides.
A program may use at most 128 MiB of HBM per device.

```python
import math
import jax
import jax.numpy as jnp
import numpy as np
from jax import lax

GRID = 192
BAND_DEV = 1
STEPS = 2
GROUPS = 4
BANDS = 4


def draw_orbitals(key, part):
    shape = (BANDS, GRID, GRID, GRID)
    return jnp.clip(jax.random.normal(key, shape, jnp.float32), -6.0, 6.0)


def plant(entries, own_key, smallest, high):
    shape = entries.shape
    place = [jax.random.randint(jax.random.fold_in(own_key, axis), (), 0, shape[axis]) for axis in range(len(shape))]
    entries = entries.at[tuple(place)].set(smallest)
    longest = shape.index(max(shape))
    place[longest] = (place[longest] + 1) % shape[longest]
    return entries.at[tuple(place)].set(high)


def setup_inputs(seed: int = 0) -> dict:
    key_list = jax.random.split(jax.random.key(seed), 3)
    orbitals = draw_orbitals(jax.random.fold_in(key_list[2], 71), 0)
    occupations = plant(jax.random.randint(key_list[1], (BANDS,), 1, 5), jax.random.fold_in(key_list[1], 1), 1, 4).astype(jnp.int32)
    return dict(orbitals=orbitals, occupations=occupations)


def screened_kernel():
    indices = jnp.arange(GRID, dtype=jnp.int32)
    folded = jnp.minimum(indices, GRID - indices)
    half_line = folded[: GRID // 2 + 1]
    squares = folded[:, None, None] ** 2 + folded[None, :, None] ** 2 + half_line[None, None, :] ** 2
    lowest = (2.0 * math.pi / GRID) ** 2
    values = 1.0 / (lowest * (1.0 + squares.astype(jnp.float32)))
    return jnp.where(squares > 0, values, jnp.zeros_like(values))


def pair_table():
    left_list, right_list, repeat_list = [], [], []
    for left_band in range(BANDS):
        for right_band in range(left_band, BANDS):
            offset = right_band // BAND_DEV - left_band // BAND_DEV
            repeats = sum(1 for shift in range(-STEPS, STEPS + 1) if (offset - shift) % GROUPS == 0)
            if repeats > 0:
                left_list.append(left_band)
                right_list.append(right_band)
                repeat_list.append(repeats)
    return (np.array(left_list, dtype=np.int32), np.array(right_list, dtype=np.int32),
            np.array(repeat_list, dtype=np.int32))


def reference(orbitals, occupations):
    kernel = screened_kernel()
    weights = occupations.astype(jnp.float32)
    left_arr, right_arr, repeat_arr = pair_table()

    def accumulate(total, item):
        left_band, right_band, repeats = item
        phi_left = lax.dynamic_index_in_dim(orbitals, left_band, 0, keepdims=False)
        phi_right = lax.dynamic_index_in_dim(orbitals, right_band, 0, keepdims=False)
        density = phi_left * phi_right
        spectrum = jnp.fft.rfftn(density)
        field = jnp.fft.irfftn(spectrum * kernel, s=(GRID, GRID, GRID)).astype(orbitals.dtype)
        scale = repeats.astype(orbitals.dtype)
        total = total.at[left_band].add(scale * weights[right_band] * phi_right * field)
        other = jnp.where(left_band != right_band, scale * weights[left_band], jnp.zeros_like(scale))
        total = total.at[right_band].add(other * phi_left * field)
        return total, None

    start = jnp.zeros(orbitals.shape, dtype=orbitals.dtype)
    total, _ = lax.scan(accumulate, start, (jnp.asarray(left_arr), jnp.asarray(right_arr), jnp.asarray(repeat_arr)))
    return -total
```

```python
import math

import jax
import jax.numpy as jnp
from jax import lax
from jax.sharding import PartitionSpec as P

STEPS = 2
PRECISION = lax.Precision.HIGH


def shifted(array, axis, by):
    length = lax.axis_size(axis)
    return lax.ppermute(array, axis, [(i, (i + by) % length) for i in range(length)])


def shifted_flat(array, axis, by):
    return shifted(array.reshape(-1, 128), axis, by).reshape(array.shape)


def hartley_table(length):
    row_index = lax.broadcasted_iota(jnp.int32, (length, length), 0)
    col_index = lax.broadcasted_iota(jnp.int32, (length, length), 1)
    phase = (row_index * col_index % length).astype(jnp.float32) * (2.0 * math.pi / length)
    return jnp.cos(phase) + jnp.sin(phase)


def folded_square(index, length):
    folded = jnp.minimum(index, length - index)
    return folded * folded


def kernel_block(length, first_row, row_count):
    shape = (length, row_count, length)
    squares = folded_square(lax.broadcasted_iota(jnp.int32, shape, 0), length)
    squares = squares + folded_square(first_row + lax.broadcasted_iota(jnp.int32, shape, 1), length)
    squares = squares + folded_square(lax.broadcasted_iota(jnp.int32, shape, 2), length)
    lowest = (2.0 * math.pi / length) ** 2
    values = 1.0 / (lowest * (1.0 + squares.astype(jnp.float32)))
    values = jnp.where(squares > 0, values, jnp.zeros_like(values))
    return (values / float(length**3)).reshape(length, row_count * length)


def along_z(field, table):
    return jnp.einsum("xyz,kz->xyk", field, table, precision=PRECISION)


def along_y(field, table):
    return jnp.einsum("xyz,ky->xkz", field, table, precision=PRECISION)


def along_x(lines, table):
    return jnp.einsum("xn,kx->kn", lines, table, precision=PRECISION)


def exchange(blocks):
    return lax.all_to_all(blocks, "space", split_axis=0, concat_axis=0, tiled=True)


def to_blocks(spectra):
    space_count = lax.axis_size("space")
    slab_rows, rows, length = spectra.shape
    blocks = spectra.reshape(slab_rows, space_count, rows // space_count * length)
    return blocks.transpose(1, 0, 2)


def from_blocks(blocks, rows):
    slab_rows = blocks.shape[1]
    return blocks.transpose(1, 0, 2).reshape(slab_rows, rows, -1)


def with_level(spectra, level):
    shape = (1,) + spectra.shape[1:]
    row = lax.broadcasted_iota(jnp.int32, shape, 1)
    column = lax.broadcasted_iota(jnp.int32, shape, 2)
    length = spectra.shape[2]
    return spectra + jnp.where((row == 0) & (column == 0), level * float(length**2), 0.0)


def solve_lines(blocks, table, kernel, holds_first):
    count, slab_rows, width = blocks.shape
    lines = blocks.reshape(count * slab_rows, width)
    first = (lax.broadcasted_iota(jnp.int32, (1, width), 1) == 0) & holds_first
    lines = lines - jnp.where(first, jnp.mean(lines[:, :1]), 0.0)
    solved = along_x(along_x(lines, table) * kernel, table)
    return solved.reshape(count, slab_rows, width)


def shards(orbitals, occupations):
    owned = orbitals[0]
    length = owned.shape[1]
    group_count = lax.axis_size("band")
    space_count = lax.axis_size("space")
    own_group = lax.axis_index("band")
    place = lax.axis_index("space")
    row_count = length // space_count
    table = hartley_table(length)
    kernel = kernel_block(length, place * row_count, row_count)
    weights = occupations.astype(jnp.float32)

    def weight(offset):
        return lax.dynamic_index_in_dim(weights, (own_group + offset) % group_count, 0, keepdims=False)

    def forward(density):
        level = jnp.mean(density)
        spectra = along_y(along_z(density - level, table), table)
        return exchange(to_blocks(with_level(spectra, level)))

    def backward(blocks):
        return along_z(along_y(from_blocks(blocks, length), table), table)

    shared = group_count == 2 * STEPS
    solo_offsets = range(1, STEPS if shared else STEPS + 1)
    guests = {offset: shifted_flat(owned, "band", -offset) for offset in range(1, STEPS + 1)}

    sent_self = forward(owned * owned)
    sent = {offset: forward(owned * guests[offset]) for offset in solo_offsets}
    if shared:
        half_rows = length // 2
        half_count = half_rows // space_count
        half = own_group // STEPS
        half_table = lax.dynamic_slice_in_dim(table, half * half_rows, half_rows, 0)
        other_table = lax.dynamic_slice_in_dim(table, (1 - half) * half_rows, half_rows, 0)
        half_kernel = kernel_block(length, half * half_rows + place * half_count, half_count)
        density = owned * guests[STEPS]
        level = jnp.mean(density)
        spectra = along_z(along_y(density - level, half_table), table)
        half_sent = exchange(to_blocks(with_level(spectra, jnp.where(half == 0, level, 0.0))))

    total = jnp.zeros_like(owned)
    returned = jnp.zeros_like(owned)
    for offset in solo_offsets:
        field = backward(exchange(solve_lines(sent[offset], table, kernel, place == 0)))
        total = total + weight(offset) * guests[offset] * field
        returned = returned + shifted_flat(weight(0) * owned * field, "band", offset)
    if shared:
        half_back = exchange(solve_lines(half_sent, table, half_kernel, (place == 0) & (half == 0)))
        other_back = shifted(half_back.reshape(-1, 128), "band", STEPS).reshape(half_back.shape)
        own_part = along_y(along_z(from_blocks(half_back, half_rows), table), half_table.T)
        other_part = along_y(along_z(from_blocks(other_back, half_rows), table), other_table.T)
        total = total + 2.0 * weight(STEPS) * guests[STEPS] * (own_part + other_part)
    field = backward(exchange(solve_lines(sent_self, table, kernel, place == 0)))
    total = total + weight(0) * owned * field
    return -(total + returned)[None]


def solution(mesh):
    placed = (P("band", "space", None, None), P())
    return jax.shard_map(
        shards,
        mesh=mesh,
        in_specs=placed,
        out_specs=P("band", "space", None, None),
        check_vma=False,
    )
```

```python
import math

import jax
import jax.numpy as jnp
from jax import lax
from jax.sharding import PartitionSpec as P

STEPS = 2
PRECISION = lax.Precision.HIGH


def moved(array, axis, targets):
    flat = lax.ppermute(array.reshape(-1, 128), axis, list(enumerate(targets)))
    return flat.reshape(array.shape)


def after(array, *earlier):
    return lax.optimization_barrier((array,) + earlier)[0]


def hartley_table(length):
    row_index = lax.broadcasted_iota(jnp.int32, (length, length), 0)
    col_index = lax.broadcasted_iota(jnp.int32, (length, length), 1)
    phase = (row_index * col_index % length).astype(jnp.float32) * (2.0 * math.pi / length)
    return jnp.cos(phase) + jnp.sin(phase)


def folded_square(index, length):
    folded = jnp.minimum(index, length - index)
    return folded * folded


def kernel_block(length, first_row, row_count):
    shape = (length, row_count, length)
    squares = folded_square(lax.broadcasted_iota(jnp.int32, shape, 0), length)
    squares = squares + folded_square(first_row + lax.broadcasted_iota(jnp.int32, shape, 1), length)
    squares = squares + folded_square(lax.broadcasted_iota(jnp.int32, shape, 2), length)
    lowest = (2.0 * math.pi / length) ** 2
    values = 1.0 / (lowest * (1.0 + squares.astype(jnp.float32)))
    values = jnp.where(squares > 0, values, jnp.zeros_like(values))
    return (values / float(length**3)).reshape(length, row_count * length)


def along_z(field, table):
    return jnp.einsum("xyz,kz->xyk", field, table, precision=PRECISION)


def along_y(field, table):
    return jnp.einsum("xyz,ky->xkz", field, table, precision=PRECISION)


def along_x(lines, table):
    return jnp.einsum("xn,kx->kn", lines, table, precision=PRECISION)


def exchange(blocks):
    return lax.all_to_all(blocks, "space", split_axis=0, concat_axis=0, tiled=True)


def to_blocks(spectra):
    space_count = lax.axis_size("space")
    slab_rows, rows, length = spectra.shape
    blocks = spectra.reshape(slab_rows, space_count, rows // space_count * length)
    return blocks.transpose(1, 0, 2)


def from_blocks(blocks, rows):
    slab_rows = blocks.shape[1]
    return blocks.transpose(1, 0, 2).reshape(slab_rows, rows, -1)


def with_level(spectra, level):
    shape = (1,) + spectra.shape[1:]
    row = lax.broadcasted_iota(jnp.int32, shape, 1)
    column = lax.broadcasted_iota(jnp.int32, shape, 2)
    length = spectra.shape[2]
    return spectra + jnp.where((row == 0) & (column == 0), level * float(length**2), 0.0)


def solve_lines(blocks, table, kernel, holds_first):
    count, slab_rows, width = blocks.shape
    lines = blocks.reshape(count * slab_rows, width)
    first = (lax.broadcasted_iota(jnp.int32, (1, width), 1) == 0) & holds_first
    lines = lines - jnp.where(first, jnp.mean(lines[:, :1]), 0.0)
    solved = along_x(along_x(lines, table) * kernel, table)
    return solved.reshape(count, slab_rows, width)


def shards(orbitals, occupations):
    owned = orbitals[0]
    length = owned.shape[1]
    group_count = lax.axis_size("band")
    space_count = lax.axis_size("space")
    own_group = lax.axis_index("band")
    place = lax.axis_index("space")
    row_count = length // space_count
    table = hartley_table(length)
    kernel = kernel_block(length, place * row_count, row_count)
    weights = occupations.astype(jnp.float32)

    def pick(values):
        return jnp.asarray(values)[own_group]

    def weight(groups):
        return weights[pick(groups)]

    def multiplicity(groups):
        counts = [
            sum((j - i - s) % group_count == 0 for s in range(-STEPS, STEPS + 1))
            for i, j in enumerate(groups)
        ]
        return pick(jnp.asarray(counts, jnp.float32))

    def forward(density):
        level = jnp.mean(density)
        spectra = along_y(along_z(density - level, table), table)
        return to_blocks(with_level(spectra, level))

    def backward(blocks):
        return along_z(along_y(from_blocks(blocks, length), table), table)

    shared = group_count == 2 * STEPS == 4
    if shared:
        ring = [0, 1, 3, 2]
        solo = [[ring[(ring.index(g) + 1) % 4] for g in range(4)]]
        opposite = [ring[(ring.index(g) + 2) % 4] for g in range(4)]
    else:
        solo = [[(g + s) % group_count for g in range(group_count)] for s in range(1, STEPS + 1)]

    def inverse(groups):
        return [groups.index(g) for g in range(group_count)]

    groups = list(range(group_count))
    guests = []
    source = owned
    for partners in solo:
        guests.append(moved(source, "band", inverse(partners)))
        source = after(owned, guests[-1])
    if shared:
        far_guest = moved(source, "band", opposite)

    arrived = exchange(forward(owned * owned))
    lines_self = arrived
    solo_lines = []
    for guest in guests:
        arrived = exchange(after(forward(owned * guest), arrived))
        solo_lines.append(arrived)
    if shared:
        half_rows = length // 2
        half_count = half_rows // space_count
        half = own_group // 2
        half_table = lax.dynamic_slice_in_dim(table, half * half_rows, half_rows, 0)
        other_table = lax.dynamic_slice_in_dim(table, (1 - half) * half_rows, half_rows, 0)
        half_kernel = kernel_block(length, half * half_rows + place * half_count, half_count)
        density = owned * far_guest
        level = jnp.mean(density)
        spectra = along_z(along_y(density - level, half_table), table)
        blocks = to_blocks(with_level(spectra, jnp.where(half == 0, level, 0.0)))
        arrived = exchange(after(blocks, arrived))
        half_lines = arrived

    total = jnp.zeros_like(owned)
    for partners, guest, lines in zip(solo, guests, solo_lines):
        solved = solve_lines(lines, table, kernel, place == 0)
        arrived = exchange(after(solved, arrived))
        field = multiplicity(partners) * backward(arrived)
        total = total + weight(partners) * guest * field
        total = total + moved(weight(groups) * owned * field, "band", partners)
    if shared:
        solved = solve_lines(half_lines, table, half_kernel, (place == 0) & (half == 0))
        arrived = exchange(after(solved, arrived))
        half_back = arrived
        other_back = moved(half_back, "band", opposite)
        own_part = along_y(along_z(from_blocks(half_back, half_rows), table), half_table.T)
        other_part = along_y(along_z(from_blocks(other_back, half_rows), table), other_table.T)
        scale = multiplicity(opposite) * weight(opposite)
        total = total + scale * far_guest * (own_part + other_part)
    solved = solve_lines(lines_self, table, kernel, place == 0)
    field = backward(exchange(after(solved, arrived)))
    return -(total + weight(groups) * owned * field)[None]


def solution(mesh):
    placed = (P("band", "space", None, None), P())
    return jax.shard_map(
        shards,
        mesh=mesh,
        in_specs=placed,
        out_specs=P("band", "space", None, None),
        check_vma=False,
    )
```

```python
import math

import jax
import jax.numpy as jnp
from jax import lax
from jax.sharding import PartitionSpec as P

STEPS = 2
PRECISION = lax.Precision.HIGH


def moved(flat, axis, targets):
    return lax.ppermute(flat, axis, list(enumerate(targets)))


def flattened(array):
    return array.reshape(-1, 128)


def after(array, *earlier):
    return lax.optimization_barrier((array,) + earlier)[0]


def hartley_table(length):
    row_index = lax.broadcasted_iota(jnp.int32, (length, length), 0)
    col_index = lax.broadcasted_iota(jnp.int32, (length, length), 1)
    phase = (row_index * col_index % length).astype(jnp.float32) * (2.0 * math.pi / length)
    return jnp.cos(phase) + jnp.sin(phase)


def folded_square(index, length):
    folded = jnp.minimum(index, length - index)
    return folded * folded


def kernel_block(length, first_row, row_count):
    shape = (length, row_count, length)
    squares = folded_square(lax.broadcasted_iota(jnp.int32, shape, 0), length)
    squares = squares + folded_square(first_row + lax.broadcasted_iota(jnp.int32, shape, 1), length)
    squares = squares + folded_square(lax.broadcasted_iota(jnp.int32, shape, 2), length)
    lowest = (2.0 * math.pi / length) ** 2
    values = 1.0 / (lowest * (1.0 + squares.astype(jnp.float32)))
    values = jnp.where(squares > 0, values, jnp.zeros_like(values))
    return (values / float(length**3)).reshape(length, row_count * length)


def along_z(field, table):
    return jnp.einsum("xyz,kz->xyk", field, table, precision=PRECISION)


def along_y(field, table):
    return jnp.einsum("xyz,ky->xkz", field, table, precision=PRECISION)


def along_x(lines, table):
    return jnp.einsum("xn,kx->kn", lines, table, precision=PRECISION)


def exchange(blocks):
    return lax.all_to_all(blocks, "space", split_axis=0, concat_axis=0, tiled=True)


def to_blocks(spectra):
    space_count = lax.axis_size("space")
    slab_rows, rows, length = spectra.shape
    blocks = spectra.reshape(slab_rows, space_count, rows // space_count * length)
    return blocks.transpose(1, 0, 2)


def from_blocks(blocks, rows):
    slab_rows = blocks.shape[1]
    return blocks.transpose(1, 0, 2).reshape(slab_rows, rows, -1)


def with_level(spectra, level):
    shape = (1,) + spectra.shape[1:]
    row = lax.broadcasted_iota(jnp.int32, shape, 1)
    column = lax.broadcasted_iota(jnp.int32, shape, 2)
    length = spectra.shape[2]
    return spectra + jnp.where((row == 0) & (column == 0), level * float(length**2), 0.0)


def solve_lines(blocks, table, kernel, holds_first):
    count, slab_rows, width = blocks.shape
    lines = blocks.reshape(count * slab_rows, width)
    first = (lax.broadcasted_iota(jnp.int32, (1, width), 1) == 0) & holds_first
    lines = lines - jnp.where(first, jnp.mean(lines[:, :1]), 0.0)
    solved = along_x(along_x(lines, table) * kernel, table)
    return solved.reshape(count, slab_rows, width)


def shards(orbitals, occupations):
    owned = orbitals[0]
    length = owned.shape[1]
    group_count = lax.axis_size("band")
    space_count = lax.axis_size("space")
    own_group = lax.axis_index("band")
    place = lax.axis_index("space")
    row_count = length // space_count
    table = hartley_table(length)
    kernel = kernel_block(length, place * row_count, row_count)
    weights = occupations.astype(jnp.float32)

    def pick(values):
        return jnp.asarray(values)[own_group]

    def weight(groups):
        return weights[pick(groups)]

    def multiplicity(groups):
        counts = [
            sum((j - i - s) % group_count == 0 for s in range(-STEPS, STEPS + 1))
            for i, j in enumerate(groups)
        ]
        return pick(jnp.asarray(counts, jnp.float32))

    def forward(density):
        level = jnp.mean(density)
        spectra = along_y(along_z(density - level, table), table)
        return to_blocks(with_level(spectra, level))

    def backward(blocks):
        return along_z(along_y(from_blocks(blocks, length), table), table)

    shared = group_count == 2 * STEPS == 4
    if shared:
        ring = [0, 1, 3, 2]
        solo = [[ring[(ring.index(g) + 1) % 4] for g in range(4)]]
        opposite = [ring[(ring.index(g) + 2) % 4] for g in range(4)]
    else:
        solo = [[(g + s) % group_count for g in range(group_count)] for s in range(1, STEPS + 1)]

    def inverse(groups):
        return [groups.index(g) for g in range(group_count)]

    groups = list(range(group_count))
    flat_guests = []
    source = flattened(owned)
    for partners in solo + ([opposite] if shared else []):
        flat_guests.append(moved(source, "band", inverse(partners)))
        source = after(source, flat_guests[-1])

    blocks = forward(owned * owned)
    arrived = exchange(blocks)
    lines_self = arrived
    guests = []
    solo_lines = []
    for index in range(len(solo)):
        guests.append(after(flat_guests[index], blocks).reshape(owned.shape))
        blocks = after(forward(owned * guests[index]), arrived)
        arrived = exchange(blocks)
        solo_lines.append(arrived)
    if shared:
        half_rows = length // 2
        half_count = half_rows // space_count
        half = own_group // 2
        half_table = lax.dynamic_slice_in_dim(table, half * half_rows, half_rows, 0)
        other_table = lax.dynamic_slice_in_dim(table, (1 - half) * half_rows, half_rows, 0)
        half_kernel = kernel_block(length, half * half_rows + place * half_count, half_count)
        far_guest = after(flat_guests[-1], blocks).reshape(owned.shape)
        density = owned * far_guest
        level = jnp.mean(density)
        spectra = along_z(along_y(density - level, half_table), table)
        blocks = to_blocks(with_level(spectra, jnp.where(half == 0, level, 0.0)))
        arrived = exchange(after(blocks, arrived))
        half_lines = arrived

    total = jnp.zeros_like(owned)
    partials = []
    returned = []
    for partners, guest, lines in zip(solo, guests, solo_lines):
        solved = solve_lines(lines, table, kernel, place == 0)
        arrived = exchange(after(solved, arrived))
        field = multiplicity(partners) * backward(arrived)
        total = total + weight(partners) * guest * field
        partial = flattened(weight(groups) * owned * field)
        partials.append(partial)
        returned.append(moved(partial, "band", partners))
    if shared:
        solved = solve_lines(half_lines, table, half_kernel, (place == 0) & (half == 0))
        arrived = exchange(after(solved, arrived))
        half_back = arrived
        flat_back = flattened(half_back)
        other_back = moved(flat_back, "band", opposite).reshape(half_back.shape)
        partials.append(flat_back)
        own_part = along_y(along_z(from_blocks(half_back, half_rows), table), half_table.T)
        other_part = along_y(along_z(from_blocks(other_back, half_rows), table), other_table.T)
        scale = multiplicity(opposite) * weight(opposite)
        total = total + scale * far_guest * (own_part + other_part)
    solved = solve_lines(lines_self, table, kernel, place == 0)
    field = backward(exchange(after(solved, arrived, *partials)))
    for partial in returned:
        total = total + partial.reshape(owned.shape)
    return -(total + weight(groups) * owned * field)[None]


def solution(mesh):
    placed = (P("band", "space", None, None), P())
    return jax.shard_map(
        shards,
        mesh=mesh,
        in_specs=placed,
        out_specs=P("band", "space", None, None),
        check_vma=False,
    )
```

```python
import math

import jax
import jax.numpy as jnp
from jax import lax
from jax.sharding import PartitionSpec as P

STEPS = 2
PRECISION = lax.Precision.HIGH


def moved(flat, axis, targets):
    return lax.ppermute(flat, axis, list(enumerate(targets)))


def flattened(array):
    return array.reshape(-1, 128)


def after(array, *earlier):
    return lax.optimization_barrier((array,) + earlier)[0]


def hartley_table(length):
    row_index = lax.broadcasted_iota(jnp.int32, (length, length), 0)
    col_index = lax.broadcasted_iota(jnp.int32, (length, length), 1)
    phase = (row_index * col_index % length).astype(jnp.float32) * (2.0 * math.pi / length)
    return jnp.cos(phase) + jnp.sin(phase)


def folded_square(index, length):
    folded = jnp.minimum(index, length - index)
    return folded * folded


def kernel_block(length, first_row, row_count):
    shape = (length, row_count, length)
    squares = folded_square(lax.broadcasted_iota(jnp.int32, shape, 0), length)
    squares = squares + folded_square(first_row + lax.broadcasted_iota(jnp.int32, shape, 1), length)
    squares = squares + folded_square(lax.broadcasted_iota(jnp.int32, shape, 2), length)
    lowest = (2.0 * math.pi / length) ** 2
    values = 1.0 / (lowest * (1.0 + squares.astype(jnp.float32)))
    values = jnp.where(squares > 0, values, jnp.zeros_like(values))
    return (values / float(length**3)).reshape(length, row_count * length)


def along_z(field, table):
    return jnp.einsum("xyz,kz->xyk", field, table, precision=PRECISION)


def along_y(field, table):
    return jnp.einsum("xyz,ky->xkz", field, table, precision=PRECISION)


def along_x(lines, table):
    return jnp.einsum("xn,kx->kn", lines, table, precision=PRECISION)


def exchange(blocks):
    return lax.all_to_all(blocks, "space", split_axis=0, concat_axis=0, tiled=True)


def to_blocks(spectra):
    space_count = lax.axis_size("space")
    slab_rows, rows, length = spectra.shape
    blocks = spectra.reshape(slab_rows, space_count, rows // space_count * length)
    return blocks.transpose(1, 0, 2)


def from_blocks(blocks, rows):
    slab_rows = blocks.shape[1]
    return blocks.transpose(1, 0, 2).reshape(slab_rows, rows, -1)


def with_level(spectra, level):
    shape = (1,) + spectra.shape[1:]
    row = lax.broadcasted_iota(jnp.int32, shape, 1)
    column = lax.broadcasted_iota(jnp.int32, shape, 2)
    length = spectra.shape[2]
    return spectra + jnp.where((row == 0) & (column == 0), level * float(length**2), 0.0)


def solve_lines(blocks, table, kernel, holds_first):
    count, slab_rows, width = blocks.shape
    lines = blocks.reshape(count * slab_rows, width)
    first = (lax.broadcasted_iota(jnp.int32, (1, width), 1) == 0) & holds_first
    lines = lines - jnp.where(first, jnp.mean(lines[:, :1]), 0.0)
    solved = along_x(along_x(lines, table) * kernel, table)
    return solved.reshape(count, slab_rows, width)


def shards(orbitals, occupations):
    owned = orbitals[0]
    length = owned.shape[1]
    group_count = lax.axis_size("band")
    space_count = lax.axis_size("space")
    own_group = lax.axis_index("band")
    place = lax.axis_index("space")
    row_count = length // space_count
    table = hartley_table(length)
    kernel = kernel_block(length, place * row_count, row_count)
    weights = occupations.astype(jnp.float32)

    def pick(values):
        return jnp.asarray(values)[own_group]

    def weight(groups):
        return weights[pick(groups)]

    def multiplicity(groups):
        counts = [
            sum((j - i - s) % group_count == 0 for s in range(-STEPS, STEPS + 1))
            for i, j in enumerate(groups)
        ]
        return pick(jnp.asarray(counts, jnp.float32))

    def forward(density):
        level = jnp.mean(density)
        spectra = along_y(along_z(density - level, table), table)
        return to_blocks(with_level(spectra, level))

    def backward(blocks):
        return along_z(along_y(from_blocks(blocks, length), table), table)

    shared = group_count == 2 * STEPS == 4
    if shared:
        ring = [0, 1, 3, 2]
        solo = [[ring[(ring.index(g) + 1) % 4] for g in range(4)]]
        opposite = [ring[(ring.index(g) + 2) % 4] for g in range(4)]
    else:
        solo = [[(g + s) % group_count for g in range(group_count)] for s in range(1, STEPS + 1)]

    def inverse(groups):
        return [groups.index(g) for g in range(group_count)]

    groups = list(range(group_count))
    early_planes = max(1, owned.shape[0] // 4)
    back = inverse(solo[0])
    early = moved(flattened(owned[:early_planes]), "band", back)
    late = moved(after(flattened(owned[early_planes:]), early), "band", back)
    flat_guests = [(early, late)]
    for partners in solo[1:] + ([opposite] if shared else []):
        source = after(flattened(owned), *flat_guests[-1])
        flat_guests.append((moved(source, "band", inverse(partners)),))

    def assembled(parts, *earlier):
        parts = lax.optimization_barrier(parts + earlier)[: len(parts)]
        return jnp.concatenate([part.reshape((-1,) + owned.shape[1:]) for part in parts])

    blocks = after(forward(owned * owned), early)
    arrived = exchange(blocks)
    lines_self = arrived
    guests = []
    solo_lines = []
    for index in range(len(solo)):
        guests.append(assembled(flat_guests[index], blocks))
        blocks = after(forward(owned * guests[index]), arrived)
        arrived = exchange(blocks)
        solo_lines.append(arrived)
    if shared:
        half_rows = length // 2
        half_count = half_rows // space_count
        half = own_group // 2
        half_table = lax.dynamic_slice_in_dim(table, half * half_rows, half_rows, 0)
        other_table = lax.dynamic_slice_in_dim(table, (1 - half) * half_rows, half_rows, 0)
        half_kernel = kernel_block(length, half * half_rows + place * half_count, half_count)
        far_guest = assembled(flat_guests[-1], blocks)
        density = owned * far_guest
        level = jnp.mean(density)
        spectra = along_z(along_y(density - level, half_table), table)
        blocks = to_blocks(with_level(spectra, jnp.where(half == 0, level, 0.0)))
        arrived = exchange(after(blocks, arrived))
        half_lines = arrived

    total = jnp.zeros_like(owned)
    if shared:
        solved = solve_lines(half_lines, table, half_kernel, (place == 0) & (half == 0))
        half_back = exchange(after(solved, arrived))
        arrived = half_back
        other_back = moved(flattened(half_back), "band", opposite).reshape(half_back.shape)
    for partners, guest, lines in zip(solo, guests, solo_lines):
        solved = solve_lines(lines, table, kernel, place == 0)
        arrived = exchange(after(solved, arrived))
        field = multiplicity(partners) * backward(arrived)
        total = total + weight(partners) * guest * field
        partial = flattened(weight(groups) * owned * field)
        total = total + moved(partial, "band", partners).reshape(owned.shape)
    if shared:
        own_part = along_y(along_z(from_blocks(half_back, half_rows), table), half_table.T)
        other_part = along_y(along_z(from_blocks(other_back, half_rows), table), other_table.T)
        scale = multiplicity(opposite) * weight(opposite)
        total = total + scale * far_guest * (own_part + other_part)
    solved = solve_lines(lines_self, table, kernel, place == 0)
    field = backward(exchange(after(solved, arrived)))
    return -(after(total) + weight(groups) * owned * field)[None]


def solution(mesh):
    placed = (P("band", "space", None, None), P())
    return jax.shard_map(
        shards,
        mesh=mesh,
        in_specs=placed,
        out_specs=P("band", "space", None, None),
        check_vma=False,
    )
```

```python
import math

import jax
import jax.numpy as jnp
from jax import lax
from jax.sharding import PartitionSpec as P

STEPS = 2
PRECISION = lax.Precision.HIGH


def moved(flat, axis, targets):
    return lax.ppermute(flat, axis, list(enumerate(targets)))


def flattened(array):
    return array.reshape(-1, 128)


def after(array, *earlier):
    return lax.optimization_barrier((array,) + earlier)[0]


def hartley_table(length):
    row_index = lax.broadcasted_iota(jnp.int32, (length, length), 0)
    col_index = lax.broadcasted_iota(jnp.int32, (length, length), 1)
    phase = (row_index * col_index % length).astype(jnp.float32) * (2.0 * math.pi / length)
    return jnp.cos(phase) + jnp.sin(phase)


def folded_square(index, length):
    folded = jnp.minimum(index, length - index)
    return folded * folded


def kernel_block(length, first_row, row_count):
    shape = (length, row_count, length)
    squares = folded_square(lax.broadcasted_iota(jnp.int32, shape, 0), length)
    squares = squares + folded_square(first_row + lax.broadcasted_iota(jnp.int32, shape, 1), length)
    squares = squares + folded_square(lax.broadcasted_iota(jnp.int32, shape, 2), length)
    lowest = (2.0 * math.pi / length) ** 2
    values = 1.0 / (lowest * (1.0 + squares.astype(jnp.float32)))
    values = jnp.where(squares > 0, values, jnp.zeros_like(values))
    return (values / float(length**3)).reshape(length, row_count * length)


def along_z(field, table):
    return jnp.einsum("xyz,kz->xyk", field, table, precision=PRECISION)


def along_y(field, table):
    return jnp.einsum("xyz,ky->xkz", field, table, precision=PRECISION)


def along_x(lines, table):
    return jnp.einsum("xn,kx->kn", lines, table, precision=PRECISION)


def exchange(blocks):
    return lax.all_to_all(blocks, "space", split_axis=0, concat_axis=0, tiled=True)


def to_blocks(spectra):
    space_count = lax.axis_size("space")
    slab_rows, rows, length = spectra.shape
    blocks = spectra.reshape(slab_rows, space_count, rows // space_count * length)
    return blocks.transpose(1, 0, 2)


def from_blocks(blocks, rows):
    slab_rows = blocks.shape[1]
    return blocks.transpose(1, 0, 2).reshape(slab_rows, rows, -1)


def with_level(spectra, level):
    shape = (1,) + spectra.shape[1:]
    row = lax.broadcasted_iota(jnp.int32, shape, 1)
    column = lax.broadcasted_iota(jnp.int32, shape, 2)
    length = spectra.shape[2]
    return spectra + jnp.where((row == 0) & (column == 0), level * float(length**2), 0.0)


def solve_lines(blocks, table, kernel, holds_first):
    count, slab_rows, width = blocks.shape
    lines = blocks.reshape(count * slab_rows, width)
    first = (lax.broadcasted_iota(jnp.int32, (1, width), 1) == 0) & holds_first
    lines = lines - jnp.where(first, jnp.mean(lines[:, :1]), 0.0)
    solved = along_x(along_x(lines, table) * kernel, table)
    return solved.reshape(count, slab_rows, width)


def shards(orbitals, occupations):
    owned = orbitals[0]
    length = owned.shape[1]
    group_count = lax.axis_size("band")
    space_count = lax.axis_size("space")
    own_group = lax.axis_index("band")
    place = lax.axis_index("space")
    row_count = length // space_count
    table = hartley_table(length)
    kernel = kernel_block(length, place * row_count, row_count)
    weights = occupations.astype(jnp.float32)

    def pick(values):
        return jnp.asarray(values)[own_group]

    def weight(groups):
        return weights[pick(groups)]

    def multiplicity(groups):
        counts = [
            sum((j - i - s) % group_count == 0 for s in range(-STEPS, STEPS + 1))
            for i, j in enumerate(groups)
        ]
        return pick(jnp.asarray(counts, jnp.float32))

    def forward(density):
        level = jnp.mean(density)
        spectra = along_y(along_z(density - level, table), table)
        return to_blocks(with_level(spectra, level))

    def backward(blocks):
        return along_z(along_y(from_blocks(blocks, length), table), table)

    shared = group_count == 2 * STEPS == 4
    if shared:
        ring = [0, 1, 3, 2]
        solo = [[ring[(ring.index(g) + 1) % 4] for g in range(4)]]
        opposite = [ring[(ring.index(g) + 2) % 4] for g in range(4)]
    else:
        solo = [[(g + s) % group_count for g in range(group_count)] for s in range(1, STEPS + 1)]

    def inverse(groups):
        return [groups.index(g) for g in range(group_count)]

    groups = list(range(group_count))
    early_planes = max(1, owned.shape[0] // 4)
    early_part = flattened(owned[:early_planes])
    late_part = flattened(owned[early_planes:])
    flat_guests = []
    last = ()
    for partners in solo + ([opposite] if shared else []):
        early = moved(after(early_part, *last), "band", inverse(partners))
        late = moved(after(late_part, early), "band", inverse(partners))
        flat_guests.append((early, late))
        last = (late,)

    def assembled(parts, *earlier):
        parts = lax.optimization_barrier(parts + earlier)[: len(parts)]
        return jnp.concatenate([part.reshape((-1,) + owned.shape[1:]) for part in parts])

    blocks = after(forward(owned * owned), flat_guests[0][0])
    arrived = exchange(blocks)
    lines_self = arrived
    guests = []
    solo_lines = []
    for index in range(len(solo)):
        guests.append(assembled(flat_guests[index], blocks))
        early = [parts[0] for parts in flat_guests[index + 1 : index + 2]]
        blocks = after(forward(owned * guests[index]), arrived, *early)
        arrived = exchange(blocks)
        solo_lines.append(arrived)
    if shared:
        half_rows = length // 2
        half_count = half_rows // space_count
        half = own_group // 2
        half_table = lax.dynamic_slice_in_dim(table, half * half_rows, half_rows, 0)
        other_table = lax.dynamic_slice_in_dim(table, (1 - half) * half_rows, half_rows, 0)
        half_kernel = kernel_block(length, half * half_rows + place * half_count, half_count)
        far_guest = assembled(flat_guests[-1], blocks)
        density = owned * far_guest
        level = jnp.mean(density)
        spectra = along_z(along_y(density - level, half_table), table)
        blocks = to_blocks(with_level(spectra, jnp.where(half == 0, level, 0.0)))
        arrived = exchange(after(blocks, arrived))
        half_lines = arrived

    total = jnp.zeros_like(owned)
    away = []
    returned = []
    if shared:
        solved = solve_lines(half_lines, table, half_kernel, (place == 0) & (half == 0))
        half_back = exchange(after(solved, arrived))
        arrived = half_back
        away.append(moved(flattened(half_back), "band", opposite))
        other_back = away[0].reshape(half_back.shape)
    for partners, guest, lines in zip(solo, guests, solo_lines):
        solved = solve_lines(lines, table, kernel, place == 0)
        arrived = exchange(after(solved, arrived))
        field = multiplicity(partners) * backward(after(arrived, *away))
        total = total + weight(partners) * guest * field
        partial = flattened(weight(groups) * owned * field)
        returned.append(moved(partial, "band", partners))
    if shared:
        own_part = along_y(along_z(from_blocks(half_back, half_rows), table), half_table.T)
        other_part = along_y(along_z(from_blocks(other_back, half_rows), table), other_table.T)
        scale = multiplicity(opposite) * weight(opposite)
        total = total + scale * far_guest * (own_part + other_part)
    solved = solve_lines(lines_self, table, kernel, place == 0)
    field = backward(exchange(after(solved, arrived)))
    total = after(total) + weight(groups) * owned * field
    for partial in returned:
        total = total + partial.reshape(owned.shape)
    return -total[None]


def solution(mesh):
    placed = (P("band", "space", None, None), P())
    return jax.shard_map(
        shards,
        mesh=mesh,
        in_specs=placed,
        out_specs=P("band", "space", None, None),
        check_vma=False,
    )
```

```python
import math

import jax
import jax.numpy as jnp
from jax import lax
from jax.sharding import PartitionSpec as P

STEPS = 2
PRECISION = lax.Precision.HIGH


def moved(flat, axis, targets):
    return lax.ppermute(flat, axis, list(enumerate(targets)))


def flattened(array):
    return array.reshape(-1, 128)


def after(array, *earlier):
    return lax.optimization_barrier((array,) + earlier)[0]


def hartley_table(length):
    row_index = lax.broadcasted_iota(jnp.int32, (length, length), 0)
    col_index = lax.broadcasted_iota(jnp.int32, (length, length), 1)
    phase = (row_index * col_index % length).astype(jnp.float32) * (2.0 * math.pi / length)
    return jnp.cos(phase) + jnp.sin(phase)


def folded_square(index, length):
    folded = jnp.minimum(index, length - index)
    return folded * folded


def kernel_block(length, first_row, row_count):
    shape = (length, row_count, length)
    squares = folded_square(lax.broadcasted_iota(jnp.int32, shape, 0), length)
    squares = squares + folded_square(first_row + lax.broadcasted_iota(jnp.int32, shape, 1), length)
    squares = squares + folded_square(lax.broadcasted_iota(jnp.int32, shape, 2), length)
    lowest = (2.0 * math.pi / length) ** 2
    values = 1.0 / (lowest * (1.0 + squares.astype(jnp.float32)))
    values = jnp.where(squares > 0, values, jnp.zeros_like(values))
    return (values / float(length**3)).reshape(length, row_count * length)


def along_z(field, table):
    return jnp.einsum("xyz,kz->xyk", field, table, precision=PRECISION)


def along_y(field, table):
    return jnp.einsum("xyz,ky->xkz", field, table, precision=PRECISION)


def along_x(lines, table):
    return jnp.einsum("xn,kx->kn", lines, table, precision=PRECISION)


def exchange(blocks):
    return lax.all_to_all(blocks, "space", split_axis=0, concat_axis=0, tiled=True)


def to_blocks(spectra):
    space_count = lax.axis_size("space")
    slab_rows, rows, length = spectra.shape
    blocks = spectra.reshape(slab_rows, space_count, rows // space_count * length)
    return blocks.transpose(1, 0, 2)


def from_blocks(blocks, rows):
    slab_rows = blocks.shape[1]
    return blocks.transpose(1, 0, 2).reshape(slab_rows, rows, -1)


def with_level(spectra, level):
    shape = (1,) + spectra.shape[1:]
    row = lax.broadcasted_iota(jnp.int32, shape, 1)
    column = lax.broadcasted_iota(jnp.int32, shape, 2)
    length = spectra.shape[2]
    return spectra + jnp.where((row == 0) & (column == 0), level * float(length**2), 0.0)


def solve_lines(blocks, table, kernel, holds_first):
    count, slab_rows, width = blocks.shape
    lines = blocks.reshape(count * slab_rows, width)
    first = (lax.broadcasted_iota(jnp.int32, (1, width), 1) == 0) & holds_first
    lines = lines - jnp.where(first, jnp.mean(lines[:, :1]), 0.0)
    solved = along_x(along_x(lines, table) * kernel, table)
    return solved.reshape(count, slab_rows, width)


def shards(orbitals, occupations):
    owned = orbitals[0]
    length = owned.shape[1]
    group_count = lax.axis_size("band")
    space_count = lax.axis_size("space")
    own_group = lax.axis_index("band")
    place = lax.axis_index("space")
    row_count = length // space_count
    table = hartley_table(length)
    kernel = kernel_block(length, place * row_count, row_count)
    weights = occupations.astype(jnp.float32)

    def pick(values):
        return jnp.asarray(values)[own_group]

    def weight(groups):
        return weights[pick(groups)]

    def multiplicity(groups):
        counts = [
            sum((j - i - s) % group_count == 0 for s in range(-STEPS, STEPS + 1))
            for i, j in enumerate(groups)
        ]
        return pick(jnp.asarray(counts, jnp.float32))

    def forward(density):
        level = jnp.mean(density)
        spectra = along_y(along_z(density - level, table), table)
        return to_blocks(with_level(spectra, level))

    def backward(blocks):
        return along_z(along_y(from_blocks(blocks, length), table), table)

    shared = group_count == 2 * STEPS == 4
    if shared:
        ring = [0, 1, 3, 2]
        solo = [[ring[(ring.index(g) + 1) % 4] for g in range(4)]]
        opposite = [ring[(ring.index(g) + 2) % 4] for g in range(4)]
    else:
        solo = [[(g + s) % group_count for g in range(group_count)] for s in range(1, STEPS + 1)]

    def inverse(groups):
        return [groups.index(g) for g in range(group_count)]

    groups = list(range(group_count))
    early_planes = max(1, owned.shape[0] // 4)
    early_part = flattened(owned[:early_planes])
    late_part = flattened(owned[early_planes:])
    flat_guests = []
    last = ()
    for partners in solo + ([opposite] if shared else []):
        early = moved(after(early_part, *last), "band", inverse(partners))
        late = moved(after(late_part, early), "band", inverse(partners))
        flat_guests.append((early, late))
        last = (late,)

    def assembled(parts, *earlier):
        parts = lax.optimization_barrier(parts + earlier)[: len(parts)]
        return jnp.concatenate([part.reshape((-1,) + owned.shape[1:]) for part in parts])

    density = after(owned, late_part)
    blocks = after(forward(density * density), flat_guests[0][0])
    arrived = exchange(blocks)
    lines_self = arrived
    guests = []
    solo_lines = []
    for index in range(len(solo)):
        guests.append(assembled(flat_guests[index], blocks))
        early = [parts[0] for parts in flat_guests[index + 1 : index + 2]]
        blocks = after(forward(owned * guests[index]), arrived, *early)
        arrived = exchange(blocks)
        solo_lines.append(arrived)
    if shared:
        half_rows = length // 2
        half_count = half_rows // space_count
        half = own_group // 2
        half_table = lax.dynamic_slice_in_dim(table, half * half_rows, half_rows, 0)
        other_table = lax.dynamic_slice_in_dim(table, (1 - half) * half_rows, half_rows, 0)
        half_kernel = kernel_block(length, half * half_rows + place * half_count, half_count)
        far_guest = assembled(flat_guests[-1], blocks)
        density = owned * far_guest
        level = jnp.mean(density)
        spectra = along_z(along_y(density - level, half_table), table)
        blocks = to_blocks(with_level(spectra, jnp.where(half == 0, level, 0.0)))
        arrived = exchange(after(blocks, arrived))
        half_lines = arrived

    total = jnp.zeros_like(owned)
    away = []
    returned = []
    cut = max(1, owned.shape[0] // 3)
    if shared:
        solved = solve_lines(half_lines, table, half_kernel, (place == 0) & (half == 0))
        half_back = exchange(after(solved, arrived))
        arrived = half_back
        away.append(moved(flattened(half_back), "band", opposite))
        other_back = away[0].reshape(half_back.shape)
    for partners, guest, lines in zip(solo, guests, solo_lines):
        own_scale = multiplicity(partners) * weight(groups)
        guest_scale = multiplicity(partners) * weight(partners)
        solved = solve_lines(lines, table, kernel, place == 0)
        arrived = exchange(after(solved, arrived, own_scale, guest_scale))
        earlier = away
        fields = []
        partials = []
        for first, last in ((0, cut), (cut, owned.shape[0])):
            field = backward(after(arrived, *earlier)[:, first:last])
            partial = flattened(own_scale * owned[first:last] * field)
            partials.append(moved(partial, "band", partners))
            fields.append(field)
            earlier = [partial]
        total = total + guest_scale * guest * jnp.concatenate(fields)
        returned.append(partials)
    if shared:
        own_part = along_y(along_z(from_blocks(half_back, half_rows), table), half_table.T)
        other_part = along_y(along_z(from_blocks(other_back, half_rows), table), other_table.T)
        scale = multiplicity(opposite) * weight(opposite)
        total = total + scale * far_guest * (own_part + other_part)
    solved = solve_lines(lines_self, table, kernel, place == 0)
    field = backward(exchange(after(solved, arrived)))
    total = after(total) + weight(groups) * owned * field
    for partials in returned:
        parts = lax.optimization_barrier((*partials, field))[: len(partials)]
        parts = [part.reshape((-1,) + owned.shape[1:]) for part in parts]
        total = total + jnp.concatenate(parts)
    return -total[None]


def solution(mesh):
    placed = (P("band", "space", None, None), P())
    return jax.shard_map(
        shards,
        mesh=mesh,
        in_specs=placed,
        out_specs=P("band", "space", None, None),
        check_vma=False,
    )
```

```python
import math

import jax
import jax.numpy as jnp
from jax import lax
from jax.sharding import PartitionSpec as P

STEPS = 2
PRECISION = lax.Precision.HIGH


def moved(flat, axis, targets):
    return lax.ppermute(flat, axis, list(enumerate(targets)))


def flattened(array):
    return array.reshape(-1, 128)


def after(array, *earlier):
    return lax.optimization_barrier((array,) + earlier)[0]


def hartley_table(length):
    row_index = lax.broadcasted_iota(jnp.int32, (length, length), 0)
    col_index = lax.broadcasted_iota(jnp.int32, (length, length), 1)
    phase = (row_index * col_index % length).astype(jnp.float32) * (2.0 * math.pi / length)
    return jnp.cos(phase) + jnp.sin(phase)


def folded_square(index, length):
    folded = jnp.minimum(index, length - index)
    return folded * folded


def kernel_block(length, first_row, row_count):
    shape = (length, row_count, length)
    squares = folded_square(lax.broadcasted_iota(jnp.int32, shape, 0), length)
    squares = squares + folded_square(first_row + lax.broadcasted_iota(jnp.int32, shape, 1), length)
    squares = squares + folded_square(lax.broadcasted_iota(jnp.int32, shape, 2), length)
    lowest = (2.0 * math.pi / length) ** 2
    values = 1.0 / (lowest * (1.0 + squares.astype(jnp.float32)))
    values = jnp.where(squares > 0, values, jnp.zeros_like(values))
    return (values / float(length**3)).reshape(length, row_count * length)


def along_z(field, table):
    return jnp.einsum("xyz,kz->xyk", field, table, precision=PRECISION)


def along_y(field, table):
    return jnp.einsum("xyz,ky->xkz", field, table, precision=PRECISION)


def along_x(lines, table):
    return jnp.einsum("xn,kx->kn", lines, table, precision=PRECISION)


def exchange(blocks):
    return lax.all_to_all(blocks, "space", split_axis=0, concat_axis=0, tiled=True)


def to_blocks(spectra):
    space_count = lax.axis_size("space")
    slab_rows, rows, length = spectra.shape
    blocks = spectra.reshape(slab_rows, space_count, rows // space_count * length)
    return blocks.transpose(1, 0, 2)


def from_blocks(blocks, rows):
    slab_rows = blocks.shape[1]
    return blocks.transpose(1, 0, 2).reshape(slab_rows, rows, -1)


def with_level(spectra, level):
    shape = (1,) + spectra.shape[1:]
    row = lax.broadcasted_iota(jnp.int32, shape, 1)
    column = lax.broadcasted_iota(jnp.int32, shape, 2)
    length = spectra.shape[2]
    return spectra + jnp.where((row == 0) & (column == 0), level * float(length**2), 0.0)


def solve_lines(blocks, table, kernel, holds_first):
    count, slab_rows, width = blocks.shape
    lines = blocks.reshape(count * slab_rows, width)
    first = (lax.broadcasted_iota(jnp.int32, (1, width), 1) == 0) & holds_first
    lines = lines - jnp.where(first, jnp.mean(lines[:, :1]), 0.0)
    solved = along_x(along_x(lines, table) * kernel, table)
    return solved.reshape(count, slab_rows, width)


def shards(orbitals, occupations):
    owned = orbitals[0]
    length = owned.shape[1]
    group_count = lax.axis_size("band")
    space_count = lax.axis_size("space")
    own_group = lax.axis_index("band")
    place = lax.axis_index("space")
    row_count = length // space_count
    table = hartley_table(length)
    kernel = kernel_block(length, place * row_count, row_count)
    weights = occupations.astype(jnp.float32)

    def pick(values):
        return jnp.asarray(values)[own_group]

    def weight(groups):
        return weights[pick(groups)]

    def multiplicity(groups):
        counts = [
            sum((j - i - s) % group_count == 0 for s in range(-STEPS, STEPS + 1))
            for i, j in enumerate(groups)
        ]
        return pick(jnp.asarray(counts, jnp.float32))

    def forward(density):
        level = jnp.mean(density)
        spectra = along_y(along_z(density - level, table), table)
        return to_blocks(with_level(spectra, level))

    def backward(blocks):
        return along_z(along_y(from_blocks(blocks, length), table), table)

    shared = group_count == 2 * STEPS == 4
    if shared:
        ring = [0, 1, 3, 2]
        solo = [[ring[(ring.index(g) + 1) % 4] for g in range(4)]]
        opposite = [ring[(ring.index(g) + 2) % 4] for g in range(4)]
    else:
        solo = [[(g + s) % group_count for g in range(group_count)] for s in range(1, STEPS + 1)]

    def inverse(groups):
        return [groups.index(g) for g in range(group_count)]

    groups = list(range(group_count))
    early_planes = max(1, owned.shape[0] // 4)
    early_part = flattened(owned[:early_planes])
    late_part = flattened(owned[early_planes:])
    flat_guests = []
    last = ()
    for partners in solo + ([opposite] if shared else []):
        early = moved(after(early_part, *last), "band", inverse(partners))
        late = moved(after(late_part, early), "band", inverse(partners))
        flat_guests.append((early, late))
        last = (late,)

    def assembled(parts, *earlier):
        parts = lax.optimization_barrier(parts + earlier)[: len(parts)]
        return jnp.concatenate([part.reshape((-1,) + owned.shape[1:]) for part in parts])

    density = after(owned, late_part)
    blocks = after(forward(density * density), flat_guests[0][0])
    arrived = exchange(blocks)
    lines_self = arrived
    guests = []
    solo_lines = []
    for index in range(len(solo)):
        guests.append(assembled(flat_guests[index], blocks))
        early = [parts[0] for parts in flat_guests[index + 1 : index + 2]]
        blocks = after(forward(owned * guests[index]), arrived, *early)
        arrived = exchange(blocks)
        solo_lines.append(arrived)
    if shared:
        half_rows = length // 2
        half_count = half_rows // space_count
        half = own_group // 2
        half_table = lax.dynamic_slice_in_dim(table, half * half_rows, half_rows, 0)
        other_table = lax.dynamic_slice_in_dim(table, (1 - half) * half_rows, half_rows, 0)
        half_kernel = kernel_block(length, half * half_rows + place * half_count, half_count)
        far_guest = assembled(flat_guests[-1], blocks)
        density = owned * far_guest
        level = jnp.mean(density)
        spectra = along_z(along_y(density - level, half_table), table)
        blocks = to_blocks(with_level(spectra, jnp.where(half == 0, level, 0.0)))
        arrived = exchange(after(blocks, arrived))
        half_lines = arrived

    total = jnp.zeros_like(owned)
    away = []
    returned = []
    cut = max(1, owned.shape[0] // 3)
    if shared:
        solved = solve_lines(half_lines, table, half_kernel, (place == 0) & (half == 0))
        half_back = exchange(after(solved, arrived))
        arrived = half_back
        away.append(moved(flattened(half_back), "band", opposite))
        other_back = away[0].reshape(half_back.shape)
    for partners, guest, lines in zip(solo, guests, solo_lines):
        own_scale = multiplicity(partners) * weight(groups)
        guest_scale = multiplicity(partners) * weight(partners)
        solved = solve_lines(lines, table, kernel, place == 0)
        arrived = exchange(after(solved, arrived, own_scale, guest_scale))
        earlier = away
        fields = []
        partials = []
        for first, last in ((0, cut), (cut, owned.shape[0])):
            field = backward(after(arrived, *earlier)[:, first:last])
            partial = flattened(own_scale * owned[first:last] * field)
            partials.append(moved(after(partial, *partials), "band", partners))
            fields.append(field)
            earlier = [partial]
        total = total + guest_scale * guest * jnp.concatenate(fields)
        returned.append(partials)
    if shared:
        own_part = along_y(along_z(from_blocks(half_back, half_rows), table), half_table.T)
        other_part = along_y(along_z(from_blocks(other_back, half_rows), table), other_table.T)
        scale = multiplicity(opposite) * weight(opposite)
        total = total + scale * far_guest * (own_part + other_part)
    solved = solve_lines(lines_self, table, kernel, place == 0)
    field = backward(exchange(after(solved, arrived)))
    total = after(total) + weight(groups) * owned * field
    for partials in returned:
        parts = lax.optimization_barrier((*partials, field))[: len(partials)]
        parts = [part.reshape((-1,) + owned.shape[1:]) for part in parts]
        total = total + jnp.concatenate(parts)
    return -total[None]


def solution(mesh):
    placed = (P("band", "space", None, None), P())
    return jax.shard_map(
        shards,
        mesh=mesh,
        in_specs=placed,
        out_specs=P("band", "space", None, None),
        check_vma=False,
    )
```
